32 devices in a mesh: dp: 8 (over z, y), fsdp: 4 (over x, core).
Axes of the slice: x: 2, y: 2, z: 4, core: 2. Of those that a mesh axis runs over, the one named last changes fastest.
Arguments:
- hidden: bfloat16 [32, 256, 1152], P(('dp', 'fsdp')), may hold values from -6 to 6
- attn_out: bfloat16 [32, 256, 1152], P(('dp', 'fsdp')), may hold values from -6 to 6
- proj_weight: bfloat16 [1152, 1152], P('fsdp'), may hold values from -0.1875 to 0.1875
- norm_gain: float32 [1152], replicated, may hold values from 0.1 to 1.9
- norm_bias: float32 [1152], replicated, may hold values from -3 to 3
- feature_cot: bfloat16 [8, 1024, 1152], P('dp', 'fsdp'), may hold values from -6 to 6
Outputs:
- features: bfloat16 [8, 1024, 1152], P('dp', 'fsdp')
- grad_hidden: bfloat16 [32, 256, 1152], P(('dp', 'fsdp'))
- grad_attn: bfloat16 [32, 256, 1152], P(('dp', 'fsdp'))
- grad_weight: bfloat16 [1152, 1152], P('fsdp')
The draws below stay inside these ranges and needn't reach their ends.
All inputs are finite; a program needn't handle non-finite values.
Results may differ from the reference program's by a relative error of at most 0.018.
Values may be sent and summed in bfloat16 or wider, within the bound.
A program may use at most 64 MiB of HBM per device.

```python
import math
import jax
import jax.numpy as jnp
from jax import lax

D = 1152
PATCHES = 256
IMG_DEV = 1
IMAGES = 32
TOKENS = 8192
SEQ = 1024
N_DP = 8
N_FSDP = 4


def with_spikes(array, stream_key, source, target, blocks, factor):
    owner, partner = [(jnp.arange(array.shape[axis_at]) // (array.shape[axis_at] // blocks)).reshape([-1 if axis == axis_at else 1 for axis in range(array.ndim)]) for axis_at in (source, target)]
    chosen = jax.random.permutation(stream_key, blocks)[partner]
    strong = (owner == chosen) | (owner == (partner + blocks // 2) % blocks)
    return jnp.where(strong, factor * array, array)


def level_of(stream_key, shape, cuts, low, top_value):
    gain = 1.0
    for dim, parts in cuts:
        heights = jax.random.uniform(jax.random.fold_in(jax.random.fold_in(stream_key, 6), dim), (parts,), jnp.float32, low / len(cuts), top_value / len(cuts))
        gain = gain * jnp.repeat(jnp.exp(heights), shape[dim] // parts).reshape((-1,) + (1,) * (len(shape) - 1 - dim))
    return gain


def centred(key, dims, width, bound, shards=(), dtype=jnp.bfloat16):
    result = width * jax.random.normal(key, dims, jnp.float32)
    if shards:
        result = result * level_of(key, dims, shards, -0.22, 0.18)
    return jnp.clip(result, -bound, bound).astype(dtype)


def noise_with(stream_key, dims, deviation, bound, pieces, heavy, dtype=jnp.bfloat16):
    array = deviation * jax.random.normal(stream_key, dims, jnp.float32)
    if pieces:
        array = array * level_of(stream_key, dims, pieces, -0.22, 0.18)
    return jnp.clip(with_spikes(array, jax.random.fold_in(stream_key, 3), *heavy), -bound, bound).astype(dtype)


def setup_inputs(seed: int = 0) -> dict:
    keys = jax.random.split(jax.random.key(seed), 7)
    hidden = centred(keys[0], (IMAGES, PATCHES, D), 1.0, 6.0, ((0, 32),))
    attn_out = noise_with(keys[1], (IMAGES, PATCHES, D), 1.0, 6.0, ((0, 32),), (0, 2, 32, 2.75))
    proj_weight = centred(keys[2], (D, D), D ** -0.5, 0.1875, ((0, 4),))
    norm_gain = jnp.clip(1.0 + 0.18 * jax.random.normal(keys[3], (D,), jnp.float32), 0.1, 1.9)
    norm_bias = centred(keys[4], (D,), 0.5, 3.0, (), jnp.float32)
    feature_cot = centred(keys[5], (N_DP, SEQ, D), 1.0, 6.0, ((0, 8), (1, 4)))
    return {"hidden": hidden, "attn_out": attn_out, "proj_weight": proj_weight, "norm_gain": norm_gain, "norm_bias": norm_bias, "feature_cot": feature_cot}


def reference(hidden, attn_out, proj_weight, norm_gain, norm_bias, feature_cot):
    attn_rows = attn_out.reshape(TOKENS, D)
    projected = jnp.dot(attn_rows, proj_weight, preferred_element_type=jnp.float32)
    stream = hidden.reshape(TOKENS, D).astype(jnp.float32) + projected
    mean_rows = lax.optimization_barrier(jnp.mean(stream, axis=-1, keepdims=True))
    centered = stream - mean_rows
    variance = lax.optimization_barrier(jnp.mean(centered * centered, axis=-1, keepdims=True))
    inverse = lax.rsqrt(variance + 1e-06)
    normed = centered * inverse
    features = (normed * norm_gain + norm_bias).astype(jnp.bfloat16)
    group_images = IMG_DEV * N_FSDP
    block = PATCHES // N_FSDP
    features = features.reshape(N_DP, group_images, N_FSDP, block, D)
    features = jnp.transpose(features, (0, 2, 1, 3, 4)).reshape(N_DP, SEQ, D)
    cot = feature_cot.reshape(N_DP, N_FSDP, group_images, block, D)
    cot = jnp.transpose(cot, (0, 2, 1, 3, 4)).reshape(TOKENS, D)
    scaled = cot.astype(jnp.float32) * norm_gain
    grad_stream = inverse * (scaled - lax.optimization_barrier(jnp.mean(scaled, axis=-1, keepdims=True)) - normed * lax.optimization_barrier(jnp.mean(scaled * normed, axis=-1, keepdims=True)))
    grad_hidden = grad_stream.astype(jnp.bfloat16)
    grad_attn = jnp.dot(grad_hidden, proj_weight.T, preferred_element_type=jnp.float32).astype(jnp.bfloat16)
    blocks = N_DP * N_FSDP
    per_block = TOKENS // blocks
    factor = 1.0 / math.sqrt(TOKENS)

    def add_block(index, total):
        start = (index * per_block).astype(jnp.int32)
        left = lax.dynamic_slice_in_dim(attn_rows, start, per_block, 0)
        right = lax.dynamic_slice_in_dim(grad_hidden, start, per_block, 0)
        term = jnp.dot(left.T, right, preferred_element_type=jnp.float32) * factor
        return total + term.astype(jnp.bfloat16).astype(jnp.float32)
    grad_weight = lax.fori_loop(0, blocks, add_block, jnp.zeros((D, D), jnp.float32))
    return (features, grad_hidden.reshape(IMAGES, PATCHES, D), grad_attn.reshape(IMAGES, PATCHES, D), grad_weight.astype(jnp.bfloat16))
```

```python
import functools
import math

import jax
import jax.numpy as jnp
from jax import lax
from jax.experimental import pallas as pl
from jax.experimental.pallas import tpu as pltpu
from jax.sharding import PartitionSpec as P

MESH = pl.DeviceIdType.MESH
F32 = jnp.float32
BF16 = jnp.bfloat16


def column_pieces(width):
    tiles = width // 128
    return next(count for count in (3, 2, 1) if tiles % count == 0)


def semaphores(pieces):
    return 14 + 6 * pieces


def kernel(
    n, ndp, factor,
    hidden_h, attn_h, weight_h, gain, bias, cot_h,
    features_h, gh_h, ga_h, gw_h,
    hid, att, att_t, peer_t, weight, cot, proj, feat, gh, gh_peer, ga,
    far, near, x_send, x_recv, y_keep, y_send, y_recv, z_own, z_up, z_mid, gw,
    send_sem, recv_sem, local_sem,
):
    rows, width = att.shape
    shard = weight_h.shape[0]
    half = shard // 2
    block = rows // n
    pieces = column_pieces(width)
    span = width // pieces
    chain = ndp // 2
    d = lax.axis_index("dp")
    f = lax.axis_index("fsdp")
    core = f + 1 - 2 * (f % 2)
    across = (f + n // 2) % n
    diagonal = (core + n // 2) % n
    peers = (core, across, diagonal)
    bit = d % 2
    side = d + 1 - 2 * bit
    z = d // 2
    low = z < chain // 2
    step = jnp.where(low, 2, -2)
    inner = d + step
    outer = d - step
    outermost = (z == 0) | (z == chain - 1)
    middle = (z == chain // 2 - 1) | (z == chain // 2)

    def remote(src, dst, index, dev):
        return pltpu.make_async_remote_copy(
            src_ref=src, dst_ref=dst, send_sem=send_sem.at[index],
            recv_sem=recv_sem.at[index], device_id=dev, device_id_type=MESH,
        )

    def local(src, dst, index):
        return pltpu.make_async_copy(src, dst, local_sem.at[index])

    def rows_of(start, size, align):
        return pl.ds(pl.multiple_of(start, align), size)

    def shard_rows(owner):
        return rows_of(owner * shard, shard, 16)

    def half_rows(owner, which):
        return rows_of(owner * shard + which * half, half, 16)

    def block_rows(which):
        return rows_of(which * block, block, 16)

    load_att = local(attn_h, att, 0)
    load_weight = local(weight_h, weight.at[shard_rows(f)], 1)
    load_hid = local(hidden_h, hid, 2)
    load_cot = local(cot_h.at[block_rows(f)], cot.at[block_rows(f)], 3)
    loads = (load_att, load_weight, load_hid, load_cot)
    for copy in loads:
        copy.start()

    barrier = pltpu.get_barrier_semaphore()
    for peer in peers:
        pl.semaphore_signal(barrier, inc=1, device_id=(d, peer), device_id_type=MESH)
    pl.semaphore_signal(barrier, inc=1, device_id=(side, f), device_id_type=MESH)
    pl.semaphore_signal(barrier, inc=1, device_id=(inner, f), device_id_type=MESH)

    @pl.when(jnp.logical_not(outermost))
    def _():
        pl.semaphore_signal(barrier, inc=1, device_id=(outer, f), device_id_type=MESH)
        pl.semaphore_wait(barrier, len(peers) + 3)

    @pl.when(outermost)
    def _():
        pl.semaphore_wait(barrier, len(peers) + 2)

    sent = []

    def go(src, dst, index, dev):
        copy = remote(src, dst, index, dev)
        copy.start()
        sent.append(copy)

    def arrived(dst, index, dev):
        remote(dst, dst, index, dev).wait_recv()

    go(weight_h.at[rows_of(bit * half, half, 16)], weight.at[half_rows(f, bit)], 1, (d, across))
    go(weight_h, weight.at[shard_rows(f)], 0, (d, core))
    for k, peer in ((2, across), (3, diagonal), (1, core)):
        go(cot_h.at[block_rows(peer)], cot.at[block_rows(f)], 4 + k, (d, peer))

    load_att.wait()
    for start in range(0, width, 128):
        att_t[start:start + 128, :] = att[:, start:start + 128].T
    go(att_t.at[shard_rows(core)], peer_t.at[0], 8, (d, core))
    go(att_t.at[shard_rows(diagonal)], peer_t.at[1], 9, (d, core))

    first = weight.at[half_rows(across, bit)]
    arrived(first, 1, (d, across))
    go(first, first, 2, (side, f))
    go(first, first, 3, (d, core))
    second = weight.at[half_rows(across, 1 - bit)]
    arrived(second, 2, (side, f))
    go(second, second, 4, (d, core))
    load_weight.wait()
    load_hid.wait()
    arrived(weight.at[shard_rows(core)], 0, (d, core))
    arrived(weight.at[half_rows(diagonal, bit)], 3, (d, core))
    arrived(weight.at[half_rows(diagonal, 1 - bit)], 4, (d, core))

    for p in range(pieces):
        cols = slice(p * span, (p + 1) * span)
        proj[:, cols] = jnp.dot(att[...], weight[:, cols], preferred_element_type=F32)

    load_cot.wait()
    for k, peer in ((1, core), (2, across), (3, diagonal)):
        arrived(cot.at[block_rows(peer)], 4 + k, (d, peer))

    strip = 16

    def norm(index, carry):
        at = rows_of(index * strip, strip, strip)
        stream = hid[at, :].astype(F32) + proj[at, :]
        centered = stream - jnp.mean(stream, axis=-1, keepdims=True)
        variance = jnp.mean(centered * centered, axis=-1, keepdims=True)
        inverse = lax.rsqrt(variance + 1e-06)
        normed = centered * inverse
        feat[at, :] = (normed * gain[...] + bias[...]).astype(BF16)
        scaled = cot[at, :].astype(F32) * gain[...]
        grad = inverse * (
            scaled
            - jnp.mean(scaled, axis=-1, keepdims=True)
            - normed * jnp.mean(scaled * normed, axis=-1, keepdims=True)
        )
        gh[at, :] = grad.astype(BF16)
        return carry

    lax.fori_loop(0, rows // strip, norm, 0)

    go(gh, gh_peer, 10, (d, core))
    go(feat.at[block_rows(core)], features_h.at[block_rows(f)], 11, (d, core))
    store_feat = local(feat.at[block_rows(f)], features_h.at[block_rows(f)], 0)
    store_gh = local(gh, gh_h, 1)
    store_feat.start()
    store_gh.start()

    def own_term(owner, cols):
        return jnp.dot(att_t[shard_rows(owner), :], gh[:, cols], preferred_element_type=F32)

    def peer_term(slot, cols):
        return jnp.dot(peer_t[slot], gh_peer[:, cols], preferred_element_type=F32)

    spans = [slice(p * span, (p + 1) * span) for p in range(pieces)]
    for p in range(pieces):
        far[p] = own_term(across, spans[p])
    arrived(peer_t.at[0], 8, (d, core))
    arrived(peer_t.at[1], 9, (d, core))
    arrived(gh_peer, 10, (d, core))
    base = 14
    for p in range(pieces):
        x_send[p] = ((far[p] + peer_term(1, spans[p])) * factor).astype(BF16)
        go(x_send.at[p], x_recv.at[p], base + p, (d, across))
    for k, peer in ((2, across), (3, diagonal)):
        go(feat.at[block_rows(peer)], features_h.at[block_rows(f)], 10 + k, (d, peer))
    for p in range(pieces):
        near[p] = (own_term(f, spans[p]) + peer_term(0, spans[p])) * factor
    for p in range(pieces):
        ga[:, spans[p]] = lax.dot_general(
            gh[...], weight[spans[p], :], (((1,), (1,)), ((), ())), preferred_element_type=F32
        ).astype(BF16)
    store_ga = local(ga, ga_h, 2)
    store_ga.start()

    own_half = rows_of(bit * half, half, 16)
    other_half = rows_of((1 - bit) * half, half, 16)

    def result(p):
        return gw.at[own_half, spans[p]]

    def up(p):
        return remote(z_own.at[p], z_up.at[p], base + 2 * pieces + p, (inner, f))

    def mid(p):
        return remote(z_own.at[p], z_mid.at[p], base + 3 * pieces + p, (inner, f))

    def down(p):
        return remote(result(p), result(p), base + 4 * pieces + p, (outer, f))

    def gather(p):
        return remote(result(p), result(p), base + 5 * pieces + p, (side, f))

    def stage_x(p):
        arrived(x_recv.at[p], base + p, (d, across))
        y_send[p] = (near[p, other_half, :] + x_recv[p, other_half, :].astype(F32)).astype(BF16)
        go(y_send.at[p], y_recv.at[p], base + pieces + p, (side, f))
        y_keep[p] = near[p, own_half, :] + x_recv[p, own_half, :].astype(F32)

    def stage_y(p):
        arrived(y_recv.at[p], base + pieces + p, (side, f))

        @pl.when(outermost)
        def _():
            z_own[p] = (y_keep[p] + y_recv[p].astype(F32)).astype(BF16)

            @pl.when(jnp.logical_not(middle))
            def _():
                up(p).start()

            @pl.when(middle)
            def _():
                mid(p).start()

    def stage_up(p):
        @pl.when(jnp.logical_not(outermost))
        def _():
            up(p).wait_recv()
            total = y_keep[p] + y_recv[p].astype(F32) + z_up[p].astype(F32)
            z_own[p] = total.astype(BF16)

            @pl.when(jnp.logical_not(middle))
            def _():
                up(p).start()

            @pl.when(middle)
            def _():
                mid(p).start()

    def stage_mid(p):
        @pl.when(middle)
        def _():
            mid(p).wait_recv()
            total = z_own[p].astype(F32) + z_mid[p].astype(F32)
            gw[own_half, spans[p]] = total.astype(BF16)
            gather(p).start()

            @pl.when(jnp.logical_not(outermost))
            def _():
                down(p).start()

    def stage_down(p):
        @pl.when(jnp.logical_not(middle))
        def _():
            down(p).wait_recv()
            gather(p).start()

            @pl.when(jnp.logical_not(outermost))
            def _():
                down(p).start()

    def stage_gather(p):
        there = gw.at[other_half, spans[p]]
        arrived(there, base + 5 * pieces + p, (side, f))

    stages = (stage_x, stage_y, stage_up, stage_mid, stage_down, stage_gather)
    for turn in range(pieces + len(stages) - 1):
        for depth in reversed(range(len(stages))):
            if 0 <= turn - depth < pieces:
                stages[depth](turn - depth)

    store_gw = local(gw, gw_h, 3)
    store_gw.start()
    for copy in sent:
        copy.wait_send()
    for p in range(pieces):
        gather(p).wait_send()

        @pl.when(middle)
        def _():
            mid(p).wait_send()

        @pl.when(jnp.logical_not(middle))
        def _():
            up(p).wait_send()

        @pl.when(jnp.logical_not(outermost))
        def _():
            down(p).wait_send()

    for k, peer in ((1, core), (2, across), (3, diagonal)):
        arrived(features_h.at[block_rows(peer)], 10 + k, (d, peer))
    for copy in (store_feat, store_gh, store_ga, store_gw):
        copy.wait()


def fused(hidden, attn_out, proj_weight, norm_gain, norm_bias, feature_cot):
    images, patches, width = hidden.shape
    n = lax.axis_size("fsdp")
    ndp = lax.axis_size("dp")
    rows = images * patches
    shard = proj_weight.shape[0]
    factor = 1.0 / math.sqrt(rows * n * ndp)
    pieces = column_pieces(width)
    span = width // pieces
    half = shard // 2
    vmem = pltpu.VMEM
    any_spec = pl.BlockSpec(memory_space=pl.ANY)
    vmem_spec = pl.BlockSpec(memory_space=vmem)
    matrix = jax.ShapeDtypeStruct((rows, width), BF16)
    outs = pl.pallas_call(
        functools.partial(kernel, n, ndp, factor),
        out_shape=(matrix, matrix, matrix, jax.ShapeDtypeStruct((shard, width), BF16)),
        in_specs=[any_spec, any_spec, any_spec, vmem_spec, vmem_spec, any_spec],
        out_specs=(any_spec,) * 4,
        scratch_shapes=[
            vmem((rows, width), BF16),
            vmem((rows, width), BF16),
            vmem((width, rows), BF16),
            vmem((2, shard, rows), BF16),
            vmem((width, width), BF16),
            vmem((rows, width), BF16),
            vmem((rows, width), F32),
            vmem((rows, width), BF16),
            vmem((rows, width), BF16),
            vmem((rows, width), BF16),
            vmem((rows, width), BF16),
            vmem((pieces, shard, span), F32),
            vmem((pieces, shard, span), F32),
            vmem((pieces, shard, span), BF16),
            vmem((pieces, shard, span), BF16),
            vmem((pieces, half, span), F32),
            vmem((pieces, half, span), BF16),
            vmem((pieces, half, span), BF16),
            vmem((pieces, half, span), BF16),
            vmem((pieces, half, span), BF16),
            vmem((pieces, half, span), BF16),
            vmem((shard, width), BF16),
            pltpu.SemaphoreType.DMA((semaphores(pieces),)),
            pltpu.SemaphoreType.DMA((semaphores(pieces),)),
            pltpu.SemaphoreType.DMA((4,)),
        ],
        compiler_params=pltpu.CompilerParams(
            collective_id=0, has_side_effects=True, vmem_limit_bytes=40 * 1024 * 1024
        ),
        cost_estimate=pl.CostEstimate(
            flops=6 * rows * width * width, bytes_accessed=16 * rows * width, transcendentals=rows
        ),
    )(
        hidden.reshape(rows, width), attn_out.reshape(rows, width), proj_weight,
        norm_gain.reshape(1, width), norm_bias.reshape(1, width),
        feature_cot.reshape(rows, width),
    )
    shape = (images, patches, width)
    features, grad_hidden, grad_attn, grad_weight = outs
    return (
        features.reshape(1, rows, width), grad_hidden.reshape(shape),
        grad_attn.reshape(shape), grad_weight,
    )


def local(hidden, attn_out, proj_weight, norm_gain, norm_bias, feature_cot):
    images, patches, width = hidden.shape
    groups = lax.axis_size("fsdp")
    shard = proj_weight.shape[0]
    planned = (
        groups == 2 * 2 and lax.axis_size("dp") % 4 == 0 and images == 1
        and shard % 32 == 0 and width % 128 == 0 and patches % (16 * groups) == 0
    )
    if planned:
        return fused(hidden, attn_out, proj_weight, norm_gain, norm_bias, feature_cot)
    total = images * patches * lax.axis_size("dp") * groups
    factor = 1.0 / math.sqrt(total)
    rows = images * patches
    attn_rows = attn_out.reshape(rows, width)
    full_weight = lax.all_gather(proj_weight, "fsdp", axis=0, tiled=True)
    projected = jnp.dot(attn_rows, full_weight, preferred_element_type=jnp.float32)
    stream = hidden.reshape(rows, width).astype(jnp.float32) + projected
    mean_rows = jnp.mean(stream, axis=-1, keepdims=True)
    centered = stream - mean_rows
    variance = jnp.mean(centered * centered, axis=-1, keepdims=True)
    inverse = lax.rsqrt(variance + 1e-06)
    normed = centered * inverse
    local_features = (
        (normed * norm_gain + norm_bias).astype(jnp.bfloat16).reshape(images, patches, width)
    )
    moved = lax.all_to_all(local_features, "fsdp", split_axis=1, concat_axis=0, tiled=True)
    features = moved.reshape(1, rows, width)
    incoming = feature_cot.reshape(images * groups, patches // groups, width)
    returned = lax.all_to_all(incoming, "fsdp", split_axis=0, concat_axis=1, tiled=True)
    scaled = returned.reshape(rows, width).astype(jnp.float32) * norm_gain
    grad_stream = inverse * (
        scaled
        - jnp.mean(scaled, axis=-1, keepdims=True)
        - normed * jnp.mean(scaled * normed, axis=-1, keepdims=True)
    )
    grad_hidden = grad_stream.astype(jnp.bfloat16)
    grad_attn = lax.dot_general(
        grad_hidden, full_weight, (((1,), (1,)), ((), ())), preferred_element_type=jnp.float32
    ).astype(jnp.bfloat16)
    product = lax.dot_general(
        attn_rows, grad_hidden, (((0,), (0,)), ((), ())), preferred_element_type=jnp.float32
    )
    partial_rows = lax.psum_scatter(
        (product * factor).astype(jnp.bfloat16), "fsdp", scatter_dimension=0, tiled=True
    ).astype(jnp.float32)
    grad_weight = lax.psum(partial_rows, "dp").astype(jnp.bfloat16)
    return (
        features,
        grad_hidden.reshape(images, patches, width),
        grad_attn.reshape(images, patches, width),
        grad_weight,
    )


def solution(mesh):
    return jax.shard_map(
        local,
        mesh=mesh,
        in_specs=(
            P(("dp", "fsdp"), None, None),
            P(("dp", "fsdp"), None, None),
            P("fsdp", None),
            P(),
            P(),
            P("dp", "fsdp", None),
        ),
        out_specs=(
            P("dp", "fsdp", None),
            P(("dp", "fsdp"), None, None),
            P(("dp", "fsdp"), None, None),
            P("fsdp", None),
        ),
        check_vma=False,
    )
```

```python
import functools
import math

import jax
import jax.numpy as jnp
from jax import lax
from jax.experimental import pallas as pl
from jax.experimental.pallas import tpu as pltpu
from jax.sharding import PartitionSpec as P

MESH = pl.DeviceIdType.MESH
F32 = jnp.float32
BF16 = jnp.bfloat16


def column_pieces(width):
    tiles = width // 128
    return next(count for count in (3, 2, 1) if tiles % count == 0)


def part_count(half):
    return next(count for count in (3, 2, 1) if half % (16 * count) == 0)


def semaphores(pieces, parts):
    return 14 + 6 * pieces + 4 * parts


def kernel(
    n, ndp, factor,
    hidden_h, attn_h, weight_h, gain, bias, cot_h,
    features_h, gh_h, ga_h, gw_h,
    hid, att, att_t, peer_t, weight, cot, proj, feat, gh, gh_peer, ga,
    far, near, x_send, x_recv, y_keep, y_send, y_recv, z_own, z_up, z_mid, gw,
    send_sem, recv_sem, local_sem,
):
    rows, width = att.shape
    shard = weight_h.shape[0]
    half = shard // 2
    block = rows // n
    pieces = column_pieces(width)
    span = width // pieces
    chain = ndp // 2
    d = lax.axis_index("dp")
    f = lax.axis_index("fsdp")
    core = f + 1 - 2 * (f % 2)
    across = (f + n // 2) % n
    diagonal = (core + n // 2) % n
    peers = (core, across, diagonal)
    bit = d % 2
    side = d + 1 - 2 * bit
    z = d // 2
    low = z < chain // 2
    step = jnp.where(low, 2, -2)
    inner = d + step
    outer = d - step
    outermost = (z == 0) | (z == chain - 1)
    middle = (z == chain // 2 - 1) | (z == chain // 2)

    def remote(src, dst, index, dev):
        return pltpu.make_async_remote_copy(
            src_ref=src, dst_ref=dst, send_sem=send_sem.at[index],
            recv_sem=recv_sem.at[index], device_id=dev, device_id_type=MESH,
        )

    def local(src, dst, index):
        return pltpu.make_async_copy(src, dst, local_sem.at[index])

    def rows_of(start, size, align):
        return pl.ds(pl.multiple_of(start, align), size)

    def shard_rows(owner):
        return rows_of(owner * shard, shard, 16)

    parts = part_count(half)
    part = half // parts

    def part_rows(owner, which, index):
        return rows_of(owner * shard + which * half + index * part, part, 16)

    def block_rows(which):
        return rows_of(which * block, block, 16)

    load_att = local(attn_h, att, 0)
    load_weight = local(weight_h, weight.at[shard_rows(f)], 1)
    load_hid = local(hidden_h, hid, 2)
    load_cot = local(cot_h.at[block_rows(f)], cot.at[block_rows(f)], 3)
    loads = (load_att, load_weight, load_hid, load_cot)
    for copy in loads:
        copy.start()

    barrier = pltpu.get_barrier_semaphore()
    for peer in peers:
        pl.semaphore_signal(barrier, inc=1, device_id=(d, peer), device_id_type=MESH)
    pl.semaphore_signal(barrier, inc=1, device_id=(side, f), device_id_type=MESH)
    pl.semaphore_signal(barrier, inc=1, device_id=(inner, f), device_id_type=MESH)

    @pl.when(jnp.logical_not(outermost))
    def _():
        pl.semaphore_signal(barrier, inc=1, device_id=(outer, f), device_id_type=MESH)
        pl.semaphore_wait(barrier, len(peers) + 3)

    @pl.when(outermost)
    def _():
        pl.semaphore_wait(barrier, len(peers) + 2)

    sent = []
    wbase = 14 + 6 * pieces

    def go(src, dst, index, dev):
        copy = remote(src, dst, index, dev)
        copy.start()
        sent.append(copy)

    def arrived(dst, index, dev):
        remote(dst, dst, index, dev).wait_recv()

    for i in range(parts):
        source = weight_h.at[rows_of(bit * half + i * part, part, 16)]
        go(source, weight.at[part_rows(f, bit, i)], wbase + i, (d, across))
    go(weight_h, weight.at[shard_rows(f)], 0, (d, core))
    go(cot_h.at[block_rows(core)], cot.at[block_rows(f)], 5, (d, core))

    load_att.wait()
    for start in range(0, width, 128):
        att_t[start:start + 128, :] = att[:, start:start + 128].T
    go(att_t.at[shard_rows(core)], peer_t.at[0], 8, (d, core))
    go(att_t.at[shard_rows(diagonal)], peer_t.at[1], 9, (d, core))

    for i in range(parts):
        first = weight.at[part_rows(across, bit, i)]
        arrived(first, wbase + i, (d, across))
        go(first, first, wbase + parts + i, (side, f))
        go(first, first, wbase + 2 * parts + i, (d, core))
    for k, peer in ((2, across), (3, diagonal)):
        go(cot_h.at[block_rows(peer)], cot.at[block_rows(f)], 4 + k, (d, peer))
    for i in range(parts):
        second = weight.at[part_rows(across, 1 - bit, i)]
        arrived(second, wbase + parts + i, (side, f))
        go(second, second, wbase + 3 * parts + i, (d, core))
    load_weight.wait()
    load_hid.wait()
    arrived(weight.at[shard_rows(core)], 0, (d, core))
    for i in range(parts):
        arrived(weight.at[part_rows(diagonal, bit, i)], wbase + 2 * parts + i, (d, core))
    for i in range(parts):
        arrived(weight.at[part_rows(diagonal, 1 - bit, i)], wbase + 3 * parts + i, (d, core))

    for p in range(pieces):
        cols = slice(p * span, (p + 1) * span)
        proj[:, cols] = jnp.dot(att[...], weight[:, cols], preferred_element_type=F32)

    load_cot.wait()
    for k, peer in ((1, core), (2, across), (3, diagonal)):
        arrived(cot.at[block_rows(peer)], 4 + k, (d, peer))

    strip = 16

    def norm(index, carry):
        at = rows_of(index * strip, strip, strip)
        stream = hid[at, :].astype(F32) + proj[at, :]
        centered = stream - jnp.mean(stream, axis=-1, keepdims=True)
        variance = jnp.mean(centered * centered, axis=-1, keepdims=True)
        inverse = lax.rsqrt(variance + 1e-06)
        normed = centered * inverse
        feat[at, :] = (normed * gain[...] + bias[...]).astype(BF16)
        scaled = cot[at, :].astype(F32) * gain[...]
        grad = inverse * (
            scaled
            - jnp.mean(scaled, axis=-1, keepdims=True)
            - normed * jnp.mean(scaled * normed, axis=-1, keepdims=True)
        )
        gh[at, :] = grad.astype(BF16)
        return carry

    lax.fori_loop(0, rows // strip, norm, 0)

    go(gh, gh_peer, 10, (d, core))
    go(feat.at[block_rows(core)], features_h.at[block_rows(f)], 11, (d, core))
    go(feat.at[block_rows(across)], features_h.at[block_rows(f)], 12, (d, across))
    store_feat = local(feat.at[block_rows(f)], features_h.at[block_rows(f)], 0)
    store_gh = local(gh, gh_h, 1)
    store_feat.start()
    store_gh.start()

    def own_term(owner, cols):
        return jnp.dot(att_t[shard_rows(owner), :], gh[:, cols], preferred_element_type=F32)

    def peer_term(slot, cols):
        return jnp.dot(peer_t[slot], gh_peer[:, cols], preferred_element_type=F32)

    spans = [slice(p * span, (p + 1) * span) for p in range(pieces)]
    for p in range(pieces):
        far[p] = own_term(across, spans[p])
    arrived(peer_t.at[0], 8, (d, core))
    arrived(peer_t.at[1], 9, (d, core))
    arrived(gh_peer, 10, (d, core))
    base = 14
    for p in range(pieces):
        x_send[p] = ((far[p] + peer_term(1, spans[p])) * factor).astype(BF16)
        go(x_send.at[p], x_recv.at[p], base + p, (d, across))
    for p in range(pieces):
        near[p] = (own_term(f, spans[p]) + peer_term(0, spans[p])) * factor
    for p in range(pieces):
        ga[:, spans[p]] = lax.dot_general(
            gh[...], weight[spans[p], :], (((1,), (1,)), ((), ())), preferred_element_type=F32
        ).astype(BF16)
    store_ga = local(ga, ga_h, 2)
    store_ga.start()

    own_half = rows_of(bit * half, half, 16)
    other_half = rows_of((1 - bit) * half, half, 16)

    def result(p):
        return gw.at[own_half, spans[p]]

    def up(p):
        return remote(z_own.at[p], z_up.at[p], base + 2 * pieces + p, (inner, f))

    def mid(p):
        return remote(z_own.at[p], z_mid.at[p], base + 3 * pieces + p, (inner, f))

    def down(p):
        return remote(result(p), result(p), base + 4 * pieces + p, (outer, f))

    def gather(p):
        return remote(result(p), result(p), base + 5 * pieces + p, (side, f))

    def stage_x(p):
        arrived(x_recv.at[p], base + p, (d, across))
        y_send[p] = (near[p, other_half, :] + x_recv[p, other_half, :].astype(F32)).astype(BF16)
        go(y_send.at[p], y_recv.at[p], base + pieces + p, (side, f))
        y_keep[p] = near[p, own_half, :] + x_recv[p, own_half, :].astype(F32)
        if p == pieces - 1:
            go(feat.at[block_rows(diagonal)], features_h.at[block_rows(f)], 13, (d, diagonal))

    def stage_y(p):
        arrived(y_recv.at[p], base + pieces + p, (side, f))

        @pl.when(outermost)
        def _():
            z_own[p] = (y_keep[p] + y_recv[p].astype(F32)).astype(BF16)

            @pl.when(jnp.logical_not(middle))
            def _():
                up(p).start()

            @pl.when(middle)
            def _():
                mid(p).start()

    def stage_up(p):
        @pl.when(jnp.logical_not(outermost))
        def _():
            up(p).wait_recv()
            total = y_keep[p] + y_recv[p].astype(F32) + z_up[p].astype(F32)
            z_own[p] = total.astype(BF16)

            @pl.when(jnp.logical_not(middle))
            def _():
                up(p).start()

            @pl.when(middle)
            def _():
                mid(p).start()

    def stage_mid(p):
        @pl.when(middle)
        def _():
            mid(p).wait_recv()
            total = z_own[p].astype(F32) + z_mid[p].astype(F32)
            gw[own_half, spans[p]] = total.astype(BF16)
            gather(p).start()

            @pl.when(jnp.logical_not(outermost))
            def _():
                down(p).start()

    def stage_down(p):
        @pl.when(jnp.logical_not(middle))
        def _():
            down(p).wait_recv()
            gather(p).start()

            @pl.when(jnp.logical_not(outermost))
            def _():
                down(p).start()

    def stage_gather(p):
        there = gw.at[other_half, spans[p]]
        arrived(there, base + 5 * pieces + p, (side, f))

    stages = (stage_x, stage_y, stage_up, stage_mid, stage_down, stage_gather)
    for turn in range(pieces + len(stages) - 1):
        for depth in reversed(range(len(stages))):
            if 0 <= turn - depth < pieces:
                stages[depth](turn - depth)

    store_gw = local(gw, gw_h, 3)
    store_gw.start()
    for copy in sent:
        copy.wait_send()
    for p in range(pieces):
        gather(p).wait_send()

        @pl.when(middle)
        def _():
            mid(p).wait_send()

        @pl.when(jnp.logical_not(middle))
        def _():
            up(p).wait_send()

        @pl.when(jnp.logical_not(outermost))
        def _():
            down(p).wait_send()

    for k, peer in ((1, core), (2, across), (3, diagonal)):
        arrived(features_h.at[block_rows(peer)], 10 + k, (d, peer))
    for copy in (store_feat, store_gh, store_ga, store_gw):
        copy.wait()


def fused(hidden, attn_out, proj_weight, norm_gain, norm_bias, feature_cot):
    images, patches, width = hidden.shape
    n = lax.axis_size("fsdp")
    ndp = lax.axis_size("dp")
    rows = images * patches
    shard = proj_weight.shape[0]
    factor = 1.0 / math.sqrt(rows * n * ndp)
    pieces = column_pieces(width)
    span = width // pieces
    half = shard // 2
    vmem = pltpu.VMEM
    any_spec = pl.BlockSpec(memory_space=pl.ANY)
    hbm_spec = pl.BlockSpec(memory_space=pltpu.HBM)
    vmem_spec = pl.BlockSpec(memory_space=vmem)
    matrix = jax.ShapeDtypeStruct((rows, width), BF16)
    outs = pl.pallas_call(
        functools.partial(kernel, n, ndp, factor),
        out_shape=(matrix, matrix, matrix, jax.ShapeDtypeStruct((shard, width), BF16)),
        in_specs=[hbm_spec, hbm_spec, hbm_spec, vmem_spec, vmem_spec, hbm_spec],
        out_specs=(any_spec,) * 4,
        scratch_shapes=[
            vmem((rows, width), BF16),
            vmem((rows, width), BF16),
            vmem((width, rows), BF16),
            vmem((2, shard, rows), BF16),
            vmem((width, width), BF16),
            vmem((rows, width), BF16),
            vmem((rows, width), F32),
            vmem((rows, width), BF16),
            vmem((rows, width), BF16),
            vmem((rows, width), BF16),
            vmem((rows, width), BF16),
            vmem((pieces, shard, span), F32),
            vmem((pieces, shard, span), F32),
            vmem((pieces, shard, span), BF16),
            vmem((pieces, shard, span), BF16),
            vmem((pieces, half, span), F32),
            vmem((pieces, half, span), BF16),
            vmem((pieces, half, span), BF16),
            vmem((pieces, half, span), BF16),
            vmem((pieces, half, span), BF16),
            vmem((pieces, half, span), BF16),
            vmem((shard, width), BF16),
            pltpu.SemaphoreType.DMA((semaphores(pieces, part_count(half)),)),
            pltpu.SemaphoreType.DMA((semaphores(pieces, part_count(half)),)),
            pltpu.SemaphoreType.DMA((4,)),
        ],
        compiler_params=pltpu.CompilerParams(
            collective_id=0, has_side_effects=True, vmem_limit_bytes=60 * 1024 * 1024
        ),
        cost_estimate=pl.CostEstimate(
            flops=6 * rows * width * width, bytes_accessed=16 * rows * width, transcendentals=rows
        ),
    )(
        hidden.reshape(rows, width), attn_out.reshape(rows, width), proj_weight,
        norm_gain.reshape(1, width), norm_bias.reshape(1, width),
        feature_cot.reshape(rows, width),
    )
    shape = (images, patches, width)
    features, grad_hidden, grad_attn, grad_weight = outs
    return (
        features.reshape(1, rows, width), grad_hidden.reshape(shape),
        grad_attn.reshape(shape), grad_weight,
    )


def local(hidden, attn_out, proj_weight, norm_gain, norm_bias, feature_cot):
    images, patches, width = hidden.shape
    groups = lax.axis_size("fsdp")
    shard = proj_weight.shape[0]
    planned = (
        groups == 2 * 2 and lax.axis_size("dp") % 4 == 0 and images == 1
        and shard % 32 == 0 and width % 128 == 0 and patches % (16 * groups) == 0
    )
    if planned:
        return fused(hidden, attn_out, proj_weight, norm_gain, norm_bias, feature_cot)
    total = images * patches * lax.axis_size("dp") * groups
    factor = 1.0 / math.sqrt(total)
    rows = images * patches
    attn_rows = attn_out.reshape(rows, width)
    full_weight = lax.all_gather(proj_weight, "fsdp", axis=0, tiled=True)
    projected = jnp.dot(attn_rows, full_weight, preferred_element_type=jnp.float32)
    stream = hidden.reshape(rows, width).astype(jnp.float32) + projected
    mean_rows = jnp.mean(stream, axis=-1, keepdims=True)
    centered = stream - mean_rows
    variance = jnp.mean(centered * centered, axis=-1, keepdims=True)
    inverse = lax.rsqrt(variance + 1e-06)
    normed = centered * inverse
    local_features = (
        (normed * norm_gain + norm_bias).astype(jnp.bfloat16).reshape(images, patches, width)
    )
    moved = lax.all_to_all(local_features, "fsdp", split_axis=1, concat_axis=0, tiled=True)
    features = moved.reshape(1, rows, width)
    incoming = feature_cot.reshape(images * groups, patches // groups, width)
    returned = lax.all_to_all(incoming, "fsdp", split_axis=0, concat_axis=1, tiled=True)
    scaled = returned.reshape(rows, width).astype(jnp.float32) * norm_gain
    grad_stream = inverse * (
        scaled
        - jnp.mean(scaled, axis=-1, keepdims=True)
        - normed * jnp.mean(scaled * normed, axis=-1, keepdims=True)
    )
    grad_hidden = grad_stream.astype(jnp.bfloat16)
    grad_attn = lax.dot_general(
        grad_hidden, full_weight, (((1,), (1,)), ((), ())), preferred_element_type=jnp.float32
    ).astype(jnp.bfloat16)
    product = lax.dot_general(
        attn_rows, grad_hidden, (((0,), (0,)), ((), ())), preferred_element_type=jnp.float32
    )
    partial_rows = lax.psum_scatter(
        (product * factor).astype(jnp.bfloat16), "fsdp", scatter_dimension=0, tiled=True
    ).astype(jnp.float32)
    grad_weight = lax.psum(partial_rows, "dp").astype(jnp.bfloat16)
    return (
        features,
        grad_hidden.reshape(images, patches, width),
        grad_attn.reshape(images, patches, width),
        grad_weight,
    )


def solution(mesh):
    return jax.shard_map(
        local,
        mesh=mesh,
        in_specs=(
            P(("dp", "fsdp"), None, None),
            P(("dp", "fsdp"), None, None),
            P("fsdp", None),
            P(),
            P(),
            P("dp", "fsdp", None),
        ),
        out_specs=(
            P("dp", "fsdp", None),
            P(("dp", "fsdp"), None, None),
            P(("dp", "fsdp"), None, None),
            P("fsdp", None),
        ),
        check_vma=False,
    )
```

```python
import functools
import math

import jax
import jax.numpy as jnp
from jax import lax
from jax.experimental import pallas as pl
from jax.experimental.pallas import tpu as pltpu
from jax.sharding import PartitionSpec as P

MESH = pl.DeviceIdType.MESH
F32 = jnp.float32
BF16 = jnp.bfloat16


def column_spans(width):
    tiles = width // 128
    first = (4 * tiles + 8) // 9
    second = (3 * (tiles - first) + 4) // 5
    spans, start = [], 0
    for count in (first, second, tiles - first - second):
        if count:
            spans.append(slice(start, start + count * 128))
            start += count * 128
    return spans


def part_count(half):
    return next(count for count in (3, 2, 1) if half % (16 * count) == 0)


def semaphores(pieces, parts):
    return 14 + 6 * pieces + 4 * parts


def kernel(
    n, ndp, factor,
    hidden_h, attn_h, weight_h, gain, bias, cot_h,
    features_h, gh_h, ga_h, gw_h,
    hid, att, att_t, peer_t, weight, cot, proj, feat, gh, gh_peer, ga,
    far, near, x_send, x_recv, y_keep, y_send, y_recv, z_own, z_up, z_mid, gw,
    send_sem, recv_sem, local_sem,
):
    rows, width = att.shape
    shard = weight_h.shape[0]
    half = shard // 2
    block = rows // n
    spans = column_spans(width)
    pieces = len(spans)
    chain = ndp // 2
    d = lax.axis_index("dp")
    f = lax.axis_index("fsdp")
    core = f + 1 - 2 * (f % 2)
    across = (f + n // 2) % n
    diagonal = (core + n // 2) % n
    peers = (core, across, diagonal)
    bit = d % 2
    side = d + 1 - 2 * bit
    z = d // 2
    low = z < chain // 2
    step = jnp.where(low, 2, -2)
    inner = d + step
    outer = d - step
    outermost = (z == 0) | (z == chain - 1)
    middle = (z == chain // 2 - 1) | (z == chain // 2)

    def remote(src, dst, index, dev):
        return pltpu.make_async_remote_copy(
            src_ref=src, dst_ref=dst, send_sem=send_sem.at[index],
            recv_sem=recv_sem.at[index], device_id=dev, device_id_type=MESH,
        )

    def local(src, dst, index):
        return pltpu.make_async_copy(src, dst, local_sem.at[index])

    def rows_of(start, size, align):
        return pl.ds(pl.multiple_of(start, align), size)

    def shard_rows(owner):
        return rows_of(owner * shard, shard, 16)

    parts = part_count(half)
    part = half // parts

    def part_rows(owner, which, index):
        return rows_of(owner * shard + which * half + index * part, part, 16)

    def block_rows(which):
        return rows_of(which * block, block, 16)

    load_att = local(attn_h, att, 0)
    load_weight = local(weight_h, weight.at[shard_rows(f)], 1)
    load_hid = local(hidden_h, hid, 2)
    load_cot = local(cot_h.at[block_rows(f)], cot.at[block_rows(f)], 3)
    loads = (load_att, load_weight, load_hid, load_cot)
    for copy in loads:
        copy.start()

    barrier = pltpu.get_barrier_semaphore()
    for peer in peers:
        pl.semaphore_signal(barrier, inc=1, device_id=(d, peer), device_id_type=MESH)
    pl.semaphore_signal(barrier, inc=1, device_id=(side, f), device_id_type=MESH)
    pl.semaphore_signal(barrier, inc=1, device_id=(inner, f), device_id_type=MESH)

    @pl.when(jnp.logical_not(outermost))
    def _():
        pl.semaphore_signal(barrier, inc=1, device_id=(outer, f), device_id_type=MESH)
        pl.semaphore_wait(barrier, len(peers) + 3)

    @pl.when(outermost)
    def _():
        pl.semaphore_wait(barrier, len(peers) + 2)

    sent = []
    wbase = 14 + 6 * pieces

    def go(src, dst, index, dev):
        copy = remote(src, dst, index, dev)
        copy.start()
        sent.append(copy)

    def arrived(dst, index, dev):
        remote(dst, dst, index, dev).wait_recv()

    for i in range(parts):
        source = weight_h.at[rows_of(bit * half + i * part, part, 16)]
        go(source, weight.at[part_rows(f, bit, i)], wbase + i, (d, across))
    go(weight_h, weight.at[shard_rows(f)], 0, (d, core))
    go(cot_h.at[block_rows(core)], cot.at[block_rows(f)], 5, (d, core))

    load_att.wait()
    for start in range(0, width, 128):
        att_t[start:start + 128, :] = att[:, start:start + 128].T
    go(att_t.at[shard_rows(core)], peer_t.at[0], 8, (d, core))
    go(att_t.at[shard_rows(diagonal)], peer_t.at[1], 9, (d, core))

    for i in range(parts):
        first = weight.at[part_rows(across, bit, i)]
        arrived(first, wbase + i, (d, across))
        go(first, first, wbase + parts + i, (side, f))
        go(first, first, wbase + 2 * parts + i, (d, core))
    for k, peer in ((2, across), (3, diagonal)):
        go(cot_h.at[block_rows(peer)], cot.at[block_rows(f)], 4 + k, (d, peer))
    for i in range(parts):
        second = weight.at[part_rows(across, 1 - bit, i)]
        arrived(second, wbase + parts + i, (side, f))
        go(second, second, wbase + 3 * parts + i, (d, core))
    load_weight.wait()
    load_hid.wait()
    arrived(weight.at[shard_rows(core)], 0, (d, core))
    for i in range(parts):
        arrived(weight.at[part_rows(diagonal, bit, i)], wbase + 2 * parts + i, (d, core))
    for i in range(parts):
        arrived(weight.at[part_rows(diagonal, 1 - bit, i)], wbase + 3 * parts + i, (d, core))

    for p in range(pieces):
        cols = spans[p]
        proj[:, cols] = jnp.dot(att[...], weight[:, cols], preferred_element_type=F32)

    load_cot.wait()
    for k, peer in ((1, core), (2, across), (3, diagonal)):
        arrived(cot.at[block_rows(peer)], 4 + k, (d, peer))

    strip = 16

    def norm(index, carry):
        at = rows_of(index * strip, strip, strip)
        stream = hid[at, :].astype(F32) + proj[at, :]
        centered = stream - jnp.mean(stream, axis=-1, keepdims=True)
        variance = jnp.mean(centered * centered, axis=-1, keepdims=True)
        inverse = lax.rsqrt(variance + 1e-06)
        normed = centered * inverse
        feat[at, :] = (normed * gain[...] + bias[...]).astype(BF16)
        scaled = cot[at, :].astype(F32) * gain[...]
        grad = inverse * (
            scaled
            - jnp.mean(scaled, axis=-1, keepdims=True)
            - normed * jnp.mean(scaled * normed, axis=-1, keepdims=True)
        )
        gh[at, :] = grad.astype(BF16)
        return carry

    lax.fori_loop(0, rows // strip, norm, 0)

    go(gh, gh_peer, 10, (d, core))
    go(feat.at[block_rows(core)], features_h.at[block_rows(f)], 11, (d, core))
    go(feat.at[block_rows(across)], features_h.at[block_rows(f)], 12, (d, across))
    store_feat = local(feat.at[block_rows(f)], features_h.at[block_rows(f)], 0)
    store_gh = local(gh, gh_h, 1)
    store_feat.start()
    store_gh.start()

    def own_term(owner, cols):
        return jnp.dot(att_t[shard_rows(owner), :], gh[:, cols], preferred_element_type=F32)

    def peer_term(slot, cols):
        return jnp.dot(peer_t[slot], gh_peer[:, cols], preferred_element_type=F32)

    def size(p):
        return spans[p].stop - spans[p].start

    def piece(ref, p):
        return ref.at[p, :, 0:size(p)]

    for p in range(pieces):
        far[p, :, 0:size(p)] = own_term(across, spans[p])
    arrived(peer_t.at[0], 8, (d, core))
    arrived(peer_t.at[1], 9, (d, core))
    arrived(gh_peer, 10, (d, core))
    base = 14
    for p in range(pieces):
        x_send[p, :, 0:size(p)] = ((far[p, :, 0:size(p)] + peer_term(1, spans[p])) * factor).astype(BF16)
        go(piece(x_send, p), piece(x_recv, p), base + p, (d, across))
    for p in range(pieces):
        near[p, :, 0:size(p)] = (own_term(f, spans[p]) + peer_term(0, spans[p])) * factor
    for p in range(pieces):
        ga[:, spans[p]] = lax.dot_general(
            gh[...], weight[spans[p], :], (((1,), (1,)), ((), ())), preferred_element_type=F32
        ).astype(BF16)
    store_ga = local(ga, ga_h, 2)
    store_ga.start()

    own_half = rows_of(bit * half, half, 16)
    other_half = rows_of((1 - bit) * half, half, 16)

    def result(p):
        return gw.at[own_half, spans[p]]

    def up(p):
        return remote(piece(z_own, p), piece(z_up, p), base + 2 * pieces + p, (inner, f))

    def mid(p):
        return remote(piece(z_own, p), piece(z_mid, p), base + 3 * pieces + p, (inner, f))

    def down(p):
        return remote(result(p), result(p), base + 4 * pieces + p, (outer, f))

    def gather(p):
        return remote(result(p), result(p), base + 5 * pieces + p, (side, f))

    def stage_x(p):
        arrived(piece(x_recv, p), base + p, (d, across))
        y_send[p, :, 0:size(p)] = (near[p, other_half, 0:size(p)] + x_recv[p, other_half, 0:size(p)].astype(F32)).astype(BF16)
        go(piece(y_send, p), piece(y_recv, p), base + pieces + p, (side, f))
        y_keep[p, :, 0:size(p)] = near[p, own_half, 0:size(p)] + x_recv[p, own_half, 0:size(p)].astype(F32)
        if p == pieces - 1:
            go(feat.at[block_rows(diagonal)], features_h.at[block_rows(f)], 13, (d, diagonal))

    def stage_y(p):
        arrived(piece(y_recv, p), base + pieces + p, (side, f))

        @pl.when(outermost)
        def _():
            z_own[p, :, 0:size(p)] = (y_keep[p, :, 0:size(p)] + y_recv[p, :, 0:size(p)].astype(F32)).astype(BF16)

            @pl.when(jnp.logical_not(middle))
            def _():
                up(p).start()

            @pl.when(middle)
            def _():
                mid(p).start()

    def stage_up(p):
        @pl.when(jnp.logical_not(outermost))
        def _():
            up(p).wait_recv()
            total = y_keep[p, :, 0:size(p)] + y_recv[p, :, 0:size(p)].astype(F32) + z_up[p, :, 0:size(p)].astype(F32)
            z_own[p, :, 0:size(p)] = total.astype(BF16)

            @pl.when(jnp.logical_not(middle))
            def _():
                up(p).start()

            @pl.when(middle)
            def _():
                mid(p).start()

    def stage_mid(p):
        @pl.when(middle)
        def _():
            mid(p).wait_recv()
            total = z_own[p, :, 0:size(p)].astype(F32) + z_mid[p, :, 0:size(p)].astype(F32)
            gw[own_half, spans[p]] = total.astype(BF16)
            gather(p).start()

            @pl.when(jnp.logical_not(outermost))
            def _():
                down(p).start()

    def stage_down(p):
        @pl.when(jnp.logical_not(middle))
        def _():
            down(p).wait_recv()
            gather(p).start()

            @pl.when(jnp.logical_not(outermost))
            def _():
                down(p).start()

    def stage_gather(p):
        there = gw.at[other_half, spans[p]]
        arrived(there, base + 5 * pieces + p, (side, f))

    stages = (stage_x, stage_y, stage_up, stage_mid, stage_down, stage_gather)
    for turn in range(pieces + len(stages) - 1):
        for depth in reversed(range(len(stages))):
            if 0 <= turn - depth < pieces:
                stages[depth](turn - depth)

    store_gw = local(gw, gw_h, 3)
    store_gw.start()
    for copy in sent:
        copy.wait_send()
    for p in range(pieces):
        gather(p).wait_send()

        @pl.when(middle)
        def _():
            mid(p).wait_send()

        @pl.when(jnp.logical_not(middle))
        def _():
            up(p).wait_send()

        @pl.when(jnp.logical_not(outermost))
        def _():
            down(p).wait_send()

    for k, peer in ((1, core), (2, across), (3, diagonal)):
        arrived(features_h.at[block_rows(peer)], 10 + k, (d, peer))
    for copy in (store_feat, store_gh, store_ga, store_gw):
        copy.wait()


def fused(hidden, attn_out, proj_weight, norm_gain, norm_bias, feature_cot):
    images, patches, width = hidden.shape
    n = lax.axis_size("fsdp")
    ndp = lax.axis_size("dp")
    rows = images * patches
    shard = proj_weight.shape[0]
    factor = 1.0 / math.sqrt(rows * n * ndp)
    spans = column_spans(width)
    pieces = len(spans)
    span = spans[0].stop
    half = shard // 2
    vmem = pltpu.VMEM
    any_spec = pl.BlockSpec(memory_space=pl.ANY)
    hbm_spec = pl.BlockSpec(memory_space=pltpu.HBM)
    vmem_spec = pl.BlockSpec(memory_space=vmem)
    matrix = jax.ShapeDtypeStruct((rows, width), BF16)
    outs = pl.pallas_call(
        functools.partial(kernel, n, ndp, factor),
        out_shape=(matrix, matrix, matrix, jax.ShapeDtypeStruct((shard, width), BF16)),
        in_specs=[hbm_spec, hbm_spec, hbm_spec, vmem_spec, vmem_spec, hbm_spec],
        out_specs=(any_spec,) * 4,
        scratch_shapes=[
            vmem((rows, width), BF16),
            vmem((rows, width), BF16),
            vmem((width, rows), BF16),
            vmem((2, shard, rows), BF16),
            vmem((width, width), BF16),
            vmem((rows, width), BF16),
            vmem((rows, width), F32),
            vmem((rows, width), BF16),
            vmem((rows, width), BF16),
            vmem((rows, width), BF16),
            vmem((rows, width), BF16),
            vmem((pieces, shard, span), F32),
            vmem((pieces, shard, span), F32),
            vmem((pieces, shard, span), BF16),
            vmem((pieces, shard, span), BF16),
            vmem((pieces, half, span), F32),
            vmem((pieces, half, span), BF16),
            vmem((pieces, half, span), BF16),
            vmem((pieces, half, span), BF16),
            vmem((pieces, half, span), BF16),
            vmem((pieces, half, span), BF16),
            vmem((shard, width), BF16),
            pltpu.SemaphoreType.DMA((semaphores(pieces, part_count(half)),)),
            pltpu.SemaphoreType.DMA((semaphores(pieces, part_count(half)),)),
            pltpu.SemaphoreType.DMA((4,)),
        ],
        compiler_params=pltpu.CompilerParams(
            collective_id=0, has_side_effects=True, vmem_limit_bytes=60 * 1024 * 1024
        ),
        cost_estimate=pl.CostEstimate(
            flops=6 * rows * width * width, bytes_accessed=16 * rows * width, transcendentals=rows
        ),
    )(
        hidden.reshape(rows, width), attn_out.reshape(rows, width), proj_weight,
        norm_gain.reshape(1, width), norm_bias.reshape(1, width),
        feature_cot.reshape(rows, width),
    )
    shape = (images, patches, width)
    features, grad_hidden, grad_attn, grad_weight = outs
    return (
        features.reshape(1, rows, width), grad_hidden.reshape(shape),
        grad_attn.reshape(shape), grad_weight,
    )


def local(hidden, attn_out, proj_weight, norm_gain, norm_bias, feature_cot):
    images, patches, width = hidden.shape
    groups = lax.axis_size("fsdp")
    shard = proj_weight.shape[0]
    planned = (
        groups == 2 * 2 and lax.axis_size("dp") % 4 == 0 and images == 1
        and shard % 32 == 0 and width % 128 == 0 and patches % (16 * groups) == 0
    )
    if planned:
        return fused(hidden, attn_out, proj_weight, norm_gain, norm_bias, feature_cot)
    total = images * patches * lax.axis_size("dp") * groups
    factor = 1.0 / math.sqrt(total)
    rows = images * patches
    attn_rows = attn_out.reshape(rows, width)
    full_weight = lax.all_gather(proj_weight, "fsdp", axis=0, tiled=True)
    projected = jnp.dot(attn_rows, full_weight, preferred_element_type=jnp.float32)
    stream = hidden.reshape(rows, width).astype(jnp.float32) + projected
    mean_rows = jnp.mean(stream, axis=-1, keepdims=True)
    centered = stream - mean_rows
    variance = jnp.mean(centered * centered, axis=-1, keepdims=True)
    inverse = lax.rsqrt(variance + 1e-06)
    normed = centered * inverse
    local_features = (
        (normed * norm_gain + norm_bias).astype(jnp.bfloat16).reshape(images, patches, width)
    )
    moved = lax.all_to_all(local_features, "fsdp", split_axis=1, concat_axis=0, tiled=True)
    features = moved.reshape(1, rows, width)
    incoming = feature_cot.reshape(images * groups, patches // groups, width)
    returned = lax.all_to_all(incoming, "fsdp", split_axis=0, concat_axis=1, tiled=True)
    scaled = returned.reshape(rows, width).astype(jnp.float32) * norm_gain
    grad_stream = inverse * (
        scaled
        - jnp.mean(scaled, axis=-1, keepdims=True)
        - normed * jnp.mean(scaled * normed, axis=-1, keepdims=True)
    )
    grad_hidden = grad_stream.astype(jnp.bfloat16)
    grad_attn = lax.dot_general(
        grad_hidden, full_weight, (((1,), (1,)), ((), ())), preferred_element_type=jnp.float32
    ).astype(jnp.bfloat16)
    product = lax.dot_general(
        attn_rows, grad_hidden, (((0,), (0,)), ((), ())), preferred_element_type=jnp.float32
    )
    partial_rows = lax.psum_scatter(
        (product * factor).astype(jnp.bfloat16), "fsdp", scatter_dimension=0, tiled=True
    ).astype(jnp.float32)
    grad_weight = lax.psum(partial_rows, "dp").astype(jnp.bfloat16)
    return (
        features,
        grad_hidden.reshape(images, patches, width),
        grad_attn.reshape(images, patches, width),
        grad_weight,
    )


def solution(mesh):
    return jax.shard_map(
        local,
        mesh=mesh,
        in_specs=(
            P(("dp", "fsdp"), None, None),
            P(("dp", "fsdp"), None, None),
            P("fsdp", None),
            P(),
            P(),
            P("dp", "fsdp", None),
        ),
        out_specs=(
            P("dp", "fsdp", None),
            P(("dp", "fsdp"), None, None),
            P(("dp", "fsdp"), None, None),
            P("fsdp", None),
        ),
        check_vma=False,
    )
```
